128 devices in a mesh: tm: 4 (over z_lo, core), chan: 32 (over x, z_hi, y).
Axes of the slice: x: 4, y: 4, z: 4 (z_hi: 2, z_lo: 2; z = z_hi * 2 + z_lo), core: 2. Of those that a mesh axis runs over, the one named last changes fastest.
Arguments:
- samples: float32 [24, 1024, 8192], P('tm', 'chan'), may hold values from -48 to 48
- source_index: int32 [128], replicated, may hold values from 0 to 8191, as said below
- dead_flags: int32 [8192], replicated, may hold values 0 or 1
Outputs:
- stacks: bfloat16 [512, 2, 128, 8192], P('tm', None, None, 'chan')
The draws below stay inside these ranges and needn't reach their ends.
Inputs may be any that keep to these rules, and one draw needn't show every extreme that they name: `source_index`: 128 distinct channel numbers in no particular order; channels 0 and 8191 are always among them. `dead_flags`: 1 marks a dead channel.
All inputs are finite; a program needn't handle non-finite values.
Results may differ from the reference program's by a relative error of at most 0.0057.
Values may be sent and summed in bfloat16 or wider, within the bound.
No kernel may reach another device: no remote copies, remote signals or barrier semaphores. Data moves between devices by JAX's collectives and lax.ppermute only.
A program may use at most 192 MiB of HBM per device.

```python
import math
import jax
import jax.numpy as jnp
from jax import lax

CHANNELS = 8192
SOURCES = 128
WIN = 1024
BINS = 512
BAND = 64
WINDOWS = 24


def draw_samples(key, part):
    key = jax.random.fold_in(key, 11)
    keys = jax.random.split(key, 3)
    channel_scale = jnp.exp(jax.random.uniform(keys[0], (CHANNELS,), jnp.float32, math.log(0.3), math.log(3.0)))
    field = jax.random.truncated_normal(keys[2], -4.0, 4.0, (WINDOWS, WIN, CHANNELS), jnp.float32)
    window_scale = jnp.exp(jax.random.uniform(keys[1], (WINDOWS, 1, 1), jnp.float32, math.log(0.5), math.log(2.0)))
    return field * channel_scale * window_scale


def draw_source_index(key, part):
    key = jax.random.fold_in(key, 23)
    key_order, key_shuffle = jax.random.split(key)
    middle = jax.random.permutation(key_order, CHANNELS - 2)[:SOURCES - 2] + 1
    chosen = jnp.concatenate([jnp.array([0, CHANNELS - 1], jnp.int32), middle.astype(jnp.int32)])
    return jax.random.permutation(key_shuffle, chosen).astype(jnp.int32)


def touch_ends(values, key, smallest, high):
    spot = [jax.random.randint(jax.random.fold_in(key, axis), (), 0, length) for axis, length in enumerate(values.shape)]
    longest = values.shape.index(max(values.shape))
    next_to = spot[:longest] + [(spot[longest] + 1) % values.shape[longest]] + spot[longest + 1:]
    return values.at[tuple(spot)].set(smallest).at[tuple(next_to)].set(high)


def setup_inputs(seed: int = 0) -> dict:
    key_list = jax.random.split(jax.random.key(seed), 4)
    return {
        "samples": draw_samples(jax.random.fold_in(key_list[3], 71), 0),
        "source_index": draw_source_index(jax.random.fold_in(key_list[3], 71), 0),
        "dead_flags": touch_ends((jax.random.randint(key_list[2], (CHANNELS,), 0, 8) < 1).astype(jnp.int32), jax.random.fold_in(key_list[2], 1), 0, 1),
    }


whiten_eps = 1e-06

def dft_table():
    sample = jnp.arange(WIN, dtype=jnp.int32)
    frequency = jnp.arange(BINS, dtype=jnp.int32)
    angles = (sample[:, None] * frequency[None, :] % WIN).astype(jnp.float32) * (2.0 * math.pi / WIN)
    window_taper = 0.5 - 0.5 * jnp.cos((sample.astype(jnp.float32) + 0.5) * (2.0 * math.pi / WIN))
    return jnp.concatenate([window_taper[:, None] * jnp.cos(angles), -window_taper[:, None] * jnp.sin(angles)], axis=1)

def whiten(spectrum, live):
    halves = spectrum.reshape(spectrum.shape[0], 2, -1, BAND, spectrum.shape[2])
    band_power = lax.optimization_barrier(jnp.sum(halves * halves, axis=(1, 3))) / BAND
    factor = live[None, None, :] / jnp.sqrt(band_power + whiten_eps)
    whitened = halves * factor[:, None, :, None, :]
    return whitened.reshape(spectrum.shape[0], 2, spectrum.shape[1] // 2, spectrum.shape[2]).astype(jnp.bfloat16)

def reference(samples, source_index, dead_flags):
    live = 1.0 - dead_flags.astype(jnp.float32)
    full_table = dft_table()

    def one_window(window):
        spectrum = jnp.dot(full_table.T, window, precision=lax.Precision.HIGHEST, preferred_element_type=jnp.float32)
        return whiten(spectrum[None], live)[0]
    whitened = lax.map(one_window, samples)
    source = jnp.take(whitened, source_index, axis=3)
    bin_block = 16 if BINS % 16 == 0 else BINS

    def stack_block(offset):
        white_part = lax.dynamic_slice_in_dim(whitened, offset, bin_block, 2).astype(jnp.float32)
        source_part = lax.dynamic_slice_in_dim(source, offset, bin_block, 2).astype(jnp.float32)
        real_part = jnp.einsum('kfs,kfc->fsc', source_part[:, 0], white_part[:, 0]) + jnp.einsum('kfs,kfc->fsc', source_part[:, 1], white_part[:, 1])
        imag_part = jnp.einsum('kfs,kfc->fsc', source_part[:, 1], white_part[:, 0]) - jnp.einsum('kfs,kfc->fsc', source_part[:, 0], white_part[:, 1])
        return (jnp.stack([real_part, imag_part], axis=1) / WINDOWS).astype(jnp.bfloat16)
    starts = jnp.arange(0, BINS, bin_block, dtype=jnp.int32)
    stacked = lax.map(stack_block, starts)
    return stacked.reshape(BINS, 2, SOURCES, CHANNELS)
```

```python
import math

import jax
import jax.numpy as jnp
from jax import lax
from jax.experimental import pallas as pl
from jax.experimental.pallas import tpu as pltpu
from jax.sharding import PartitionSpec as P

WIN = 1024
BINS = 512
BAND = 64
WINDOWS = 24
SOURCES = 128
CHAN = 32
TM = 4
KW = WINDOWS // TM
SUB = WIN // CHAN
WIDTH = 256
PICK = SOURCES // CHAN
DATA = KW * SUB
ROWS = DATA + 16
GROUP = 4
DEPTH = WINDOWS * 2 * GROUP
STEPS = 128.0
TOP = 32767.0
EPS = 1e-06
VMEM = 56 * 1024 * 1024

f32 = jnp.float32
bf16 = jnp.bfloat16


def split(x):
    high = x.astype(bf16)
    return high, (x - high.astype(f32)).astype(bf16)


def dft_table():
    row = jnp.arange(2 * BINS, dtype=jnp.int32)[:, None]
    sample = jnp.arange(WIN, dtype=jnp.int32)[None, :]
    frequency = row // (2 * GROUP) * GROUP + row % GROUP
    part = row // GROUP % 2
    phase = (sample * frequency + part * (WIN // 4)) % WIN
    taper = 0.5 - 0.5 * jnp.cos((sample.astype(f32) + 0.5) * (2.0 * math.pi / WIN))
    table = taper * jnp.cos(phase.astype(f32) * (2.0 * math.pi / WIN))
    table = lax.optimization_barrier(table)
    high = lax.reduce_precision(table, 8, 7)
    return high.astype(bf16), (table - high).astype(bf16)


def scale_of(code):
    return jnp.exp2(code * (1.0 / STEPS)) * (1.0 / TOP)


def encode_kernel(samples, source, out, picked, extra):
    step = pl.program_id(0)
    wide = samples.shape[2]
    blocks = wide // WIDTH

    @pl.when(step == 0)
    def _():
        picked[...] = jnp.zeros_like(picked)
        extra[...] = jnp.zeros_like(extra)

    codes = []
    scales = []
    for w in range(KW):
        x = samples[w]
        peak = jnp.max(jnp.abs(x), axis=0, keepdims=True)
        scale = jnp.ceil(jnp.log2(jnp.maximum(peak, 1e-30)) * STEPS) + 1.0
        q = jnp.round(x * (jnp.exp2(scale * (-1.0 / STEPS)) * TOP))
        codes.append(q)
        scales.append(scale)
        qi = q.astype(jnp.int32).astype(jnp.int16)
        for k in range(blocks):
            out[step * blocks + k, w * SUB : (w + 1) * SUB, :] = qi[:, k * WIDTH : (k + 1) * WIDTH]
    scales.append(jnp.zeros((8 - KW, wide), f32))
    scale_rows = jnp.concatenate(scales, 0)
    for k in range(blocks):
        start = pl.multiple_of((step * blocks + k) * 16 + 8, 8)
        for half in range(2):
            lane = k * WIDTH + half * 128
            extra[half, pl.ds(start, 8), :] = scale_rows[:, lane : lane + 128]
    both = jnp.concatenate(codes + [scale_rows, jnp.zeros((8, wide), f32)], 0)
    high = jnp.round(both * (1.0 / 256.0))
    low = both - high * 256.0
    number = lax.broadcasted_iota(jnp.int32, (SOURCES, wide), 1) + step * wide
    chooser = jnp.where(source[...] == number, 1.0, 0.0).astype(bf16)
    over = (((1,), (1,)), ((), ()))
    picked[:, :ROWS] += 256.0 * lax.dot_general(
        chooser, high.astype(bf16), over, preferred_element_type=f32
    ) + lax.dot_general(chooser, low.astype(bf16), over, preferred_element_type=f32)

    @pl.when(step == pl.num_programs(0) - 1)
    def _():
        for half in range(2):
            lanes = slice(half * 128, half * 128 + 128)
            for k in range(PICK):
                extra[half, pl.ds(k, CHAN, stride=16), :] = picked[
                    k * CHAN : (k + 1) * CHAN, lanes
                ]
            rows = extra[half].reshape(CHAN, 16, 128)
            out[:, DATA:, lanes] = rows.astype(jnp.int32).astype(jnp.int16)


def encode(samples, source_index):
    wide = 1024
    return pl.pallas_call(
        encode_kernel,
        grid=(samples.shape[2] // wide,),
        in_specs=[
            pl.BlockSpec((KW, SUB, wide), lambda i: (0, 0, i)),
            pl.BlockSpec((SOURCES, 1), lambda i: (0, 0)),
        ],
        out_specs=pl.BlockSpec((CHAN, ROWS, WIDTH), lambda i: (0, 0, 0)),
        out_shape=jax.ShapeDtypeStruct((CHAN, ROWS, WIDTH), jnp.int16),
        scratch_shapes=[
            pltpu.VMEM((SOURCES, WIDTH), f32),
            pltpu.VMEM((2, CHAN * 16, 128), f32),
        ],
        compiler_params=pltpu.CompilerParams(vmem_limit_bytes=VMEM),
        name="encode",
    )(samples, source_index.reshape(SOURCES, 1))


def transform_kernel(mine, codes, extra, high, low, live, *rest):
    outs, (table, scale) = rest[:TM], rest[TM:]
    w = pl.program_id(0)
    rows = 2 * BAND

    @pl.when(w == 0)
    def _():
        for k in range(TM):
            other = jnp.bitwise_xor(mine[0], k)
            table[k * rows : (k + 1) * rows, :] = high[other, 0]
            table[(TM + k) * rows : (TM + k + 1) * rows, :] = low[other, 0]
        scale[...] = scale_of(extra[:, 8:, :].astype(jnp.int32).astype(f32))

    x = codes[...].astype(jnp.int32).astype(f32) * scale[:, pl.ds(w, 1), :]
    x_high, x_low = split(x.reshape(WIN, WIDTH))
    y = jnp.dot(table[...], x_high, preferred_element_type=f32)
    z = jnp.dot(table[: TM * rows, :], x_low, preferred_element_type=f32)
    for k in range(TM):
        part = slice(k * rows, (k + 1) * rows)
        value = y[part] + (y[(TM + k) * rows : (TM + k + 1) * rows] + z[part])
        power = jnp.sum(value * value, axis=0, keepdims=True) * (1.0 / BAND)
        outs[k][0] = (value * (live[...] * lax.rsqrt(power + EPS))).astype(bf16)


def transform(mine, received, high, low, live, band):
    rows = 2 * BAND
    shape = jax.ShapeDtypeStruct((KW, rows, WIDTH), bf16)
    return pl.pallas_call(
        transform_kernel,
        grid_spec=pltpu.PrefetchScalarGridSpec(
            num_scalar_prefetch=1,
            grid=(KW,),
            in_specs=[
                pl.BlockSpec((CHAN, SUB, WIDTH), lambda w, _: (0, w, 0)),
                pl.BlockSpec((CHAN, 16, WIDTH), lambda w, _: (0, DATA // 16, 0)),
                pl.BlockSpec((TM, 1, rows, WIN), lambda w, _: (0, band, 0, 0)),
                pl.BlockSpec((TM, 1, rows, WIN), lambda w, _: (0, band, 0, 0)),
                pl.BlockSpec((1, WIDTH), lambda w, _: (0, 0)),
            ],
            out_specs=[pl.BlockSpec((1, rows, WIDTH), lambda w, _: (w, 0, 0))] * TM,
            scratch_shapes=[
                pltpu.VMEM((2 * TM * rows, WIN), bf16),
                pltpu.VMEM((CHAN, 8, WIDTH), f32),
            ],
        ),
        out_shape=[shape] * TM,
        compiler_params=pltpu.CompilerParams(vmem_limit_bytes=VMEM),
        name="transform",
    )(
        mine,
        received,
        received,
        high.reshape(TM, 2, rows, WIN),
        low.reshape(TM, 2, rows, WIN),
        live,
    )


def sources_kernel(mine, x, high, low, live, *outs):
    x_high, x_low = split(x[...])
    over = (((1,), (1,)), ((), ()))
    rows = 2 * BINS // TM
    for k in range(TM):
        part = pl.ds(pl.multiple_of(jnp.bitwise_xor(mine[0], k) * rows, rows), rows)
        t_high = high[part, :]
        value = lax.dot_general(x_high, t_high, over, preferred_element_type=f32) + (
            lax.dot_general(x_high, low[part, :], over, preferred_element_type=f32)
            + lax.dot_general(x_low, t_high, over, preferred_element_type=f32)
        )
        for b in range(rows // (2 * BAND)):
            band = value[:, b * 2 * BAND : (b + 1) * 2 * BAND]
            power = jnp.sum(band * band, axis=1, keepdims=True) * (1.0 / BAND)
            outs[k][:, b * 2 * BAND : (b + 1) * 2 * BAND] = (
                band * (live[...] * lax.rsqrt(power + EPS))
            ).astype(bf16)


def sources(mine, received, high, low, live):
    extra = received[:, DATA : DATA + PICK, :].astype(f32)
    codes = extra[:, :, :DATA].reshape(CHAN, PICK, KW, SUB)
    scale = scale_of(extra[:, :, DATA + 0 : DATA + KW])
    x = (codes * scale[..., None]).transpose(2, 1, 0, 3).reshape(KW * PICK, WIN)
    rows = 2 * BINS // TM
    whole = pl.BlockSpec(memory_space=pltpu.VMEM)
    return pl.pallas_call(
        sources_kernel,
        in_specs=[pl.BlockSpec(memory_space=pltpu.SMEM)] + [whole] * 4,
        out_specs=[whole] * TM,
        out_shape=[jax.ShapeDtypeStruct((KW * PICK, rows), bf16)] * TM,
        compiler_params=pltpu.CompilerParams(vmem_limit_bytes=VMEM),
        name="sources",
    )(mine, x, high, low, live)


def arrange_kernel(gathered, out, flat, turned):
    count = TM * KW
    for half in range(2):
        lanes = slice(half * 128, half * 128 + 128)
        flat[half] = gathered[:, :, lanes].reshape(CHAN * count * PICK, 128).astype(f32)
    groups = 4 * BAND // (2 * GROUP)
    for v in range(count):
        for half in range(2):
            both = jnp.concatenate(
                [
                    flat[half, pl.ds(v * PICK + k, CHAN, stride=count * PICK), :]
                    for k in range(PICK)
                ],
                0,
            )
            turned[half * 16 : half * 16 + 16, v * 8 : v * 8 + 8, :] = both.T.reshape(16, 8, SOURCES)
    column = lax.broadcasted_iota(jnp.int32, (DEPTH, 1), 0)
    second = column // GROUP % 2 == 1

    def body(g, carry):
        value = turned[g]
        ahead = pltpu.roll(value, DEPTH - GROUP, 0)
        behind = pltpu.roll(value, GROUP, 0)
        out[g, :SOURCES, :] = value.T.astype(bf16)
        out[g, SOURCES:, :] = jnp.where(second, -behind, ahead).T.astype(bf16)
        return carry

    lax.fori_loop(0, groups, body, 0)


def arrange(gathered):
    groups = 4 * BAND // (2 * GROUP)
    whole = pl.BlockSpec(memory_space=pltpu.VMEM)
    return pl.pallas_call(
        arrange_kernel,
        in_specs=[whole],
        out_specs=whole,
        out_shape=jax.ShapeDtypeStruct((groups, 2 * SOURCES, DEPTH), bf16),
        scratch_shapes=[
            pltpu.VMEM((2, CHAN * TM * KW * PICK, 128), f32),
            pltpu.VMEM((groups, DEPTH, SOURCES), f32),
        ],
        compiler_params=pltpu.CompilerParams(vmem_limit_bytes=VMEM),
        name="arrange",
    )(gathered)


def stack_kernel(left, a, b, c, d, *rest):
    out = rest[-1]
    column = lax.broadcasted_iota(jnp.int32, (2 * SOURCES, DEPTH), 1) % GROUP
    for h in range(2):
        right = jnp.concatenate(
            [v[:, h * 8 : h * 8 + 8, :] for v in [u[...].astype(f32) for u in (a, b, c, d)]], 0
        )
        right = right.reshape(DEPTH, WIDTH).astype(bf16)
        value = left[h]
        for i in range(GROUP):
            mine = jnp.where(column == i, value, jnp.zeros_like(value))
            product = jnp.dot(mine, right, preferred_element_type=f32) * (1.0 / WINDOWS)
            out[h * GROUP + i] = product.reshape(2, SOURCES, WIDTH).astype(bf16)


def stack(left, parts, band, before):
    steps = 2 * BAND // 16
    start = band * steps
    piece = pl.BlockSpec((KW, 16, WIDTH), lambda i: (0, i, 0))
    extra = [] if before is None else [before]
    return pl.pallas_call(
        stack_kernel,
        grid=(steps,),
        in_specs=[pl.BlockSpec((2, 2 * SOURCES, DEPTH), lambda i: (start + i, 0, 0))]
        + [piece] * TM
        + [pl.BlockSpec(memory_space=pl.ANY)] * len(extra),
        out_specs=pl.BlockSpec((2 * GROUP, 2, SOURCES, WIDTH), lambda i: (start + i, 0, 0, 0)),
        out_shape=jax.ShapeDtypeStruct((BINS // TM, 2, SOURCES, WIDTH), bf16),
        input_output_aliases={} if before is None else {5: 0},
        compiler_params=pltpu.CompilerParams(vmem_limit_bytes=VMEM),
        name="stack",
    )(left, *parts, *extra)


def exchange(pieces):
    moved = [pieces[0]]
    for k in range(1, TM):
        moved.append(lax.ppermute(pieces[k], "tm", [(i, i ^ k) for i in range(TM)]))
    return moved


def shards(samples, source_index, dead_flags):
    place = lax.axis_index("chan")
    mine = lax.axis_index("tm").astype(jnp.int32).reshape(1)
    live_all = 1.0 - dead_flags.astype(f32)
    live = lax.dynamic_slice_in_dim(live_all, place * WIDTH, WIDTH).reshape(1, WIDTH)
    own_sources = lax.dynamic_slice_in_dim(source_index.reshape(PICK, CHAN), place, 1, 1)[:, 0]
    live_source = jnp.tile(live_all[own_sources], KW).reshape(KW * PICK, 1)
    high, low = dft_table()

    received = lax.all_to_all(encode(samples, source_index), "chan", 0, 0, tiled=True)
    first = exchange(transform(mine, received, high, low, live, 0))
    spectra = exchange(sources(mine, received, high, low, live_source))
    second = exchange(transform(mine, received, high, low, live, 1))
    gathered = lax.all_gather(jnp.concatenate(spectra, 0), "chan", axis=0, tiled=False)
    left = arrange(gathered)
    half = stack(left, first, 0, None)
    return stack(left, second, 1, half)


def solution(mesh):
    return jax.shard_map(
        shards,
        mesh=mesh,
        in_specs=(P("tm", "chan", None), P(), P()),
        out_specs=P("tm", None, None, "chan"),
        check_vma=False,
    )
```

```python
import functools
import math

import jax
import jax.numpy as jnp
from jax import lax
from jax.experimental import pallas as pl
from jax.experimental.pallas import tpu as pltpu
from jax.sharding import PartitionSpec as P

WIN = 1024
BINS = 512
BAND = 64
WINDOWS = 24
SOURCES = 128
CHAN = 32
TM = 4
KW = WINDOWS // TM
SUB = WIN // CHAN
WIDTH = 256
NEAR = 16
PICK = SOURCES // NEAR
DATA = KW * SUB
ROWS = DATA + 16
GROUP = 4
DEPTH = WINDOWS * 2 * GROUP
STEPS = 128.0
TOP = 32767.0
ROUND = 1.5 * 2.0**23
EPS = 1e-06
VMEM = 56 * 1024 * 1024

f32 = jnp.float32
bf16 = jnp.bfloat16


def split(x):
    high = x.astype(bf16)
    return high, (x - high.astype(f32)).astype(bf16)


def dft_table():
    row = jnp.arange(2 * BINS, dtype=jnp.int32)[:, None]
    sample = jnp.arange(WIN, dtype=jnp.int32)[None, :]
    rows = 2 * BAND
    place = row // (TM * rows) * BAND + row // rows % TM * (2 * BAND)
    frequency = place + row % rows // (2 * GROUP) * GROUP + row % GROUP
    part = row // GROUP % 2
    phase = (sample * frequency + part * (WIN // 4)) % WIN
    taper = 0.5 - 0.5 * jnp.cos((sample.astype(f32) + 0.5) * (2.0 * math.pi / WIN))
    table = taper * jnp.cos(phase.astype(f32) * (2.0 * math.pi / WIN))
    table = lax.optimization_barrier(table).reshape(2, BINS, WIN)
    high = lax.reduce_precision(table, 8, 7)
    return jnp.concatenate([high.astype(bf16), (table - high).astype(bf16)], 1)


def scale_of(code):
    return jnp.exp2(code * (1.0 / STEPS)) * (1.0 / TOP)


def encode_kernel(samples, source, result, out, picked, extra, sems):
    step = pl.program_id(0)
    wide = samples.shape[2]
    blocks = wide // WIDTH
    steps = CHAN // blocks

    def copy(i):
        here = pl.ds(i * blocks, blocks)
        return pltpu.make_async_copy(
            out.at[here, :DATA, :], result.at[here, :DATA, :], sems.at[i]
        )

    @pl.when(step == 0)
    def _():
        picked[...] = jnp.zeros_like(picked)
        extra[...] = jnp.zeros_like(extra)

    number = lax.broadcasted_iota(jnp.int32, (wide, SOURCES), 0) + step * wide
    chooser = jnp.where(source[...] == number, 1.0, 0.0).astype(bf16)
    codes = []
    scales = []
    for w in range(KW):
        x = samples[w]
        peak = jnp.max(jnp.abs(x), axis=0, keepdims=True)
        scale = jnp.ceil(jnp.log2(jnp.maximum(peak, 1e-30)) * STEPS) + 1.0
        q = (x * (jnp.exp2(scale * (-1.0 / STEPS)) * TOP) + ROUND) - ROUND
        codes.append(q)
        scales.append(scale)
        qi = q.astype(jnp.int32).astype(jnp.int16)
        for k in range(blocks):
            out[step * blocks + k, w * SUB : (w + 1) * SUB, :] = qi[:, k * WIDTH : (k + 1) * WIDTH]
    copy(step).start()
    scales = jnp.concatenate(scales + [jnp.zeros((16 - KW, wide), f32)], 0)
    for k in range(blocks):
        for half in range(2):
            lane = k * WIDTH + half * 128
            start = pl.multiple_of((step * blocks + k) * 16 + 8, 8)
            extra[half, pl.ds(start, 8), :] = scales[:8, lane : lane + 128]
    high, low = split(jnp.concatenate(codes + [scales], 0))
    both = jnp.dot(jnp.concatenate([high, low], 0), chooser, preferred_element_type=f32)
    picked[:ROWS, :] += both[:ROWS] + both[ROWS:]

    @pl.when(step == pl.num_programs(0) - 1)
    def _():
        chosen = picked[...].T
        for half in range(2):
            part = chosen[:, half * 128 : half * 128 + 128]
            for d in range(NEAR):
                for z in range(2):
                    row = (d // 4 * 8 + z * 4 + d % 4) * 16
                    extra[half, row : row + PICK, :] = part[d * PICK : (d + 1) * PICK]
            rows = extra[half].reshape(CHAN, 16, 128)
            out[:, DATA:, half * 128 : half * 128 + 128] = rows.astype(jnp.int32).astype(jnp.int16)
        last = pltpu.make_async_copy(out.at[:, DATA:, :], result.at[:, DATA:, :], sems.at[steps])
        last.start()
        for i in range(steps):
            copy(i).wait()
        last.wait()


def encode(samples, source_index):
    wide = 2048
    steps = samples.shape[2] // wide
    return pl.pallas_call(
        encode_kernel,
        grid=(steps,),
        in_specs=[
            pl.BlockSpec((KW, SUB, wide), lambda i: (0, 0, i)),
            pl.BlockSpec((1, SOURCES), lambda i: (0, 0)),
        ],
        out_specs=pl.BlockSpec(memory_space=pl.ANY),
        out_shape=jax.ShapeDtypeStruct((CHAN, ROWS, WIDTH), jnp.int16),
        scratch_shapes=[
            pltpu.VMEM((CHAN, ROWS, WIDTH), jnp.int16),
            pltpu.VMEM((WIDTH, SOURCES), f32),
            pltpu.VMEM((2, CHAN * 16, 128), f32),
            pltpu.SemaphoreType.DMA((steps + 1,)),
        ],
        compiler_params=pltpu.CompilerParams(vmem_limit_bytes=VMEM),
        name="encode",
    )(samples, source_index.reshape(1, SOURCES))


def transform_kernel(mine, codes, extra, table, live, *rest):
    outs, (scale, white) = rest[:-2], rest[-2:]
    step = pl.program_id(0)
    rows = 2 * BAND
    batch = codes.shape[1] // SUB

    @pl.when(step == 0)
    def _():
        scale[...] = scale_of(extra[...].astype(jnp.int32).astype(f32)[:, 8:, :])

    for v in range(batch):
        value = codes[:, v * SUB : (v + 1) * SUB, :].astype(jnp.int32).astype(f32)
        value = value * scale[:, pl.ds(step * batch + v, 1), :]
        high, low = split(value.reshape(WIN, WIDTH))
        y = jnp.dot(table[0], high, preferred_element_type=f32)
        z = jnp.dot(table[0, : TM * rows], low, preferred_element_type=f32)
        for k in range(TM):
            part = slice(k * rows, (k + 1) * rows)
            value = y[part] + (y[(TM + k) * rows : (TM + k + 1) * rows] + z[part])
            power = jnp.sum(value * value, axis=0, keepdims=True) * (1.0 / BAND)
            white[k] = (value * (live[...] * lax.rsqrt(power + EPS))).astype(bf16)
        for k in range(TM):
            outs[k][v * rows : (v + 1) * rows, :] = white[jnp.bitwise_xor(mine[0], k)]


def transform(mine, received, table, live, band):
    rows = 2 * BAND
    batch = 2
    piece = pl.BlockSpec((batch * rows, WIDTH), lambda w, _: (w, 0))
    out_specs = [piece] * TM
    shapes = [jax.ShapeDtypeStruct((KW * rows, WIDTH), bf16)] * TM
    return pl.pallas_call(
        transform_kernel,
        grid_spec=pltpu.PrefetchScalarGridSpec(
            num_scalar_prefetch=1,
            grid=(KW // batch,),
            in_specs=[
                pl.BlockSpec((CHAN, batch * SUB, WIDTH), lambda w, _: (0, w, 0)),
                pl.BlockSpec((CHAN, 16, WIDTH), lambda w, _: (0, DATA // 16, 0)),
                pl.BlockSpec((1, 2 * BINS, WIN), lambda w, _: (band, 0, 0)),
                pl.BlockSpec((1, WIDTH), lambda w, _: (0, 0)),
            ],
            out_specs=out_specs,
            scratch_shapes=[pltpu.VMEM((CHAN, 8, WIDTH), f32), pltpu.VMEM((TM, rows, WIDTH), bf16)],
        ),
        out_shape=shapes,
        compiler_params=pltpu.CompilerParams(vmem_limit_bytes=VMEM),
        cost_estimate=pl.CostEstimate(flops=40 * 10**9, bytes_accessed=10**8, transcendentals=0),
        name="transform",
    )(mine, received, received, table, live)


def sources_kernel(mine, extra, table, live, *rest):
    outs, (x, bands) = rest[:TM], rest[TM:]
    for first in range(0, CHAN, 4):
        values = [extra[d].astype(jnp.int32).astype(f32)[:PICK] for d in range(first, first + 4)]
        scales = [scale_of(value[:, DATA : DATA + KW]) for value in values]
        for w in range(KW):
            x[w * PICK : (w + 1) * PICK, first * SUB : (first + 4) * SUB] = jnp.concatenate(
                [
                    value[:, w * SUB : (w + 1) * SUB] * scale[:, w : w + 1]
                    for value, scale in zip(values, scales)
                ],
                1,
            )
    high, low = split(x[...])
    over = (((1,), (1,)), ((), ()))
    rows = 2 * BAND
    for b in range(2):
        y = lax.dot_general(high, table[b], over, preferred_element_type=f32)
        z = lax.dot_general(low, table[b, : TM * rows], over, preferred_element_type=f32)
        value = y[:, : TM * rows] + (y[:, TM * rows :] + z)
        for k in range(TM):
            band = value[:, k * rows : (k + 1) * rows]
            power = jnp.sum(band * band, axis=1, keepdims=True) * (1.0 / BAND)
            bands[b, k] = band * (live[...] * lax.rsqrt(power + EPS))
    for b in range(2):
        for k in range(TM):
            value = bands[b, jnp.bitwise_xor(mine[0], k)]
            outs[k][:, b * rows : (b + 1) * rows] = value.astype(bf16)


def sources(mine, received, table, live):
    rows = 2 * BAND
    piece = pl.BlockSpec((KW * PICK, WIDTH), lambda i: (0, 0))
    return pl.pallas_call(
        sources_kernel,
        grid=(1,),
        in_specs=[
            pl.BlockSpec(memory_space=pltpu.SMEM),
            pl.BlockSpec((CHAN, 16, WIDTH), lambda i: (0, DATA // 16, 0)),
            pl.BlockSpec((2, 2 * BINS, WIN), lambda i: (0, 0, 0)),
            pl.BlockSpec((KW * PICK, 1), lambda i: (0, 0)),
        ],
        out_specs=[piece] * TM,
        out_shape=[jax.ShapeDtypeStruct((KW * PICK, WIDTH), bf16)] * TM,
        scratch_shapes=[pltpu.VMEM((KW * PICK, WIN), f32), pltpu.VMEM((2, TM, KW * PICK, rows), f32)],
        compiler_params=pltpu.CompilerParams(vmem_limit_bytes=VMEM),
        name="sources",
    )(mine, received, table, live)


def pack_kernel(a, b, c, d, out):
    parts = [u[...].astype(f32) for u in (a, b, c, d)]
    rows = [part[w * PICK : (w + 1) * PICK] for part in parts for w in range(KW)]
    block = lax.broadcasted_iota(jnp.int32, (PICK, 128), 1) // (2 * GROUP)
    for band in range(2):
        tiles = []
        pieces = [row[:, band * 128 : band * 128 + 128] for row in rows]
        for g in range(16):
            tile = jnp.zeros((PICK, 128), f32)
            for v in range(16):
                tile = jnp.where(block == v, pltpu.roll(pieces[v], (v - g) * 8 % 128, 1), tile)
            tiles.append(tile)
        for g in range(8):
            tile = jnp.zeros((PICK, 128), f32)
            for v in range(16):
                shift = (v - g * 2 - v // 8) * 8 % 128
                tile = jnp.where(block == v, pltpu.roll(pieces[16 + v % 8], shift, 1), tile)
            tiles.append(tile)
        value = jnp.concatenate(tiles, 0).astype(bf16)
        for d in range(NEAR):
            out[d, band] = value


def pack(spectra):
    whole = pl.BlockSpec(memory_space=pltpu.VMEM)
    return pl.pallas_call(
        pack_kernel,
        in_specs=[whole] * TM,
        out_specs=whole,
        out_shape=jax.ShapeDtypeStruct((NEAR, 2, 24 * PICK, 128), bf16),
        compiler_params=pltpu.CompilerParams(vmem_limit_bytes=VMEM),
        name="pack",
    )(*spectra)


def stack_kernel(band, sources, a, b, c, d, *rest):
    result, out, tiles, sems = rest[-4:]
    steps = BAND // GROUP // 2
    column = lax.broadcasted_iota(jnp.int32, (1, DEPTH), 1) % GROUP
    masks = [jnp.where(column == i, 1.0, 0.0).astype(bf16) for i in range(GROUP)]
    second = lax.broadcasted_iota(jnp.int32, (1, 128), 1) // GROUP % 2 == 1

    def copy(g):
        start = band * BAND + g * 2 * GROUP
        return pltpu.make_async_copy(
            out.at[pl.ds(g * 2 * GROUP, 2 * GROUP)],
            result.at[pl.ds(start, 2 * GROUP)],
            sems.at[g],
        )

    for place in range(NEAR):
        value = sources[place, 0].astype(f32).reshape(24, PICK, 128)
        tiles[:, place * PICK : (place + 1) * PICK, :] = value

    def imaginary(value):
        ahead = pltpu.roll(value, 128 - GROUP, 1)
        behind = pltpu.roll(value, GROUP, 1)
        return jnp.where(second, -behind, ahead)

    def body(g, carry):
        parts = [
            jnp.stack([u[pl.ds(pl.multiple_of(w * 2 * BAND + g * 16, 16), 16), :] for w in range(KW)])
            for u in (a, b, c, d)
        ]
        parts = [u.astype(f32) for u in parts]
        late = tiles[16 + g]
        for h in range(2):
            right = jnp.concatenate([u[:, h * 8 : h * 8 + 8, :] for u in parts], 0)
            right = right.reshape(DEPTH, WIDTH).astype(bf16)
            early = tiles[g * 2 + h]
            later = pltpu.roll(late, 64, 1) if h else late
            value = jnp.concatenate(
                [
                    jnp.concatenate([early, imaginary(early)], 0),
                    jnp.concatenate([later, imaginary(later)], 0)[:, :64],
                ],
                1,
            ).astype(bf16)
            for i in range(GROUP):
                product = jnp.dot(value * masks[i], right, preferred_element_type=f32)
                out[(g * 2 + h) * GROUP + i] = (
                    (product * (1.0 / WINDOWS)).reshape(2, SOURCES, WIDTH).astype(bf16)
                )
        copy(g).start()
        return carry

    lax.fori_loop(0, steps, body, 0)

    def finish(g, carry):
        copy(g).wait()
        return carry

    lax.fori_loop(0, steps, finish, 0)


def stack(sources, parts, band, before):
    whole = pl.BlockSpec((KW * 2 * BAND, WIDTH), lambda i: (0, 0))
    extra = [] if before is None else [before]
    return pl.pallas_call(
        functools.partial(stack_kernel, band),
        grid=(1,),
        in_specs=[pl.BlockSpec((NEAR, 1, 24 * PICK, 128), lambda i: (0, band, 0, 0))]
        + [whole] * TM
        + [pl.BlockSpec(memory_space=pl.ANY)] * len(extra),
        out_specs=pl.BlockSpec(memory_space=pl.ANY),
        out_shape=jax.ShapeDtypeStruct((BINS // TM, 2, SOURCES, WIDTH), bf16),
        scratch_shapes=[
            pltpu.VMEM((BAND, 2, SOURCES, WIDTH), bf16),
            pltpu.VMEM((24, SOURCES, 128), f32),
            pltpu.SemaphoreType.DMA((BAND // GROUP // 2,)),
        ],
        input_output_aliases={} if before is None else {1 + TM: 0},
        compiler_params=pltpu.CompilerParams(vmem_limit_bytes=VMEM),
        name="stack",
    )(sources, *parts, *extra)


def swap(value, axis, size, distance):
    return lax.ppermute(value, axis, [(i, i ^ distance) for i in range(size)])


def after(value, *others):
    return lax.optimization_barrier((value,) + others)[0]


def shards(samples, source_index, dead_flags):
    place = lax.axis_index("chan").astype(jnp.int32)
    mine = lax.axis_index("tm").astype(jnp.int32).reshape(1)
    live_all = 1.0 - dead_flags.astype(f32)
    live = lax.dynamic_slice_in_dim(live_all, place * WIDTH, WIDTH).reshape(1, WIDTH)
    place = place // 8 * 4 + place % 4
    own_sources = lax.dynamic_slice_in_dim(source_index, place * PICK, PICK)
    live_source = jnp.tile(live_all[own_sources], KW).reshape(KW * PICK, 1)
    table = dft_table()

    received = lax.all_to_all(encode(samples, source_index), "chan", 0, 0, tiled=True)
    spectra = sources(mine, received, table, live_source)
    spectra = [spectra[0]] + [swap(spectra[k], "tm", TM, k) for k in range(1, TM)]
    pieces = transform(mine, after(received, spectra[0]), table, live, 0)
    first = [pieces[0]] + [swap(after(pieces[k], *spectra[1:]), "tm", TM, k) for k in range(1, TM)]
    packed = pack([after(spectra[0], pieces[0])] + spectra[1:])
    groups = [[x * 8 + z * 4 + y for x in range(4) for y in range(4)] for z in range(2)]
    left = lax.all_to_all(packed, "chan", 0, 0, tiled=True, axis_index_groups=groups)
    pieces = transform(mine, after(received, packed), table, live, 1)
    second = [pieces[0]] + [
        swap(after(pieces[k], *first[2:]), "tm", TM, k) for k in range(1, TM)
    ]
    result = stack(left, first, 0, None)
    return stack(left, second, 1, result)


def solution(mesh):
    return jax.shard_map(
        shards,
        mesh=mesh,
        in_specs=(P("tm", "chan", None), P(), P()),
        out_specs=P("tm", None, None, "chan"),
        check_vma=False,
    )
```

```python
import functools
import math

import jax
import jax.numpy as jnp
from jax import lax
from jax.experimental import pallas as pl
from jax.experimental.pallas import tpu as pltpu
from jax.sharding import PartitionSpec as P

WIN = 1024
BINS = 512
BAND = 64
WINDOWS = 24
SOURCES = 128
CHAN = 32
TM = 4
KW = WINDOWS // TM
SUB = WIN // CHAN
WIDTH = 256
NEAR = 16
PICK = SOURCES // NEAR
DATA = KW * SUB
ROWS = DATA + 16
GROUP = 4
DEPTH = WINDOWS * 2 * GROUP
STEPS = 128.0
TOP = 32767.0
ROUND = 1.5 * 2.0**23
EPS = 1e-06
VMEM = 56 * 1024 * 1024
VMEM_LESS = 46 * 1024 * 1024
VMEM_LEAST = 40 * 1024 * 1024
LONG = pl.CostEstimate(flops=40 * 10**9, bytes_accessed=10**8, transcendentals=0)

f32 = jnp.float32
bf16 = jnp.bfloat16


def split(x):
    high = x.astype(bf16)
    return high, (x - high.astype(f32)).astype(bf16)


def dft_table():
    row = jnp.arange(2 * BINS, dtype=jnp.int32)[:, None]
    sample = jnp.arange(WIN, dtype=jnp.int32)[None, :]
    rows = 2 * BAND
    place = row // (TM * rows) * BAND + row // rows % TM * (2 * BAND)
    frequency = place + row % rows // (2 * GROUP) * GROUP + row % GROUP
    part = row // GROUP % 2
    phase = (sample * frequency + part * (WIN // 4)) % WIN
    taper = 0.5 - 0.5 * jnp.cos((sample.astype(f32) + 0.5) * (2.0 * math.pi / WIN))
    table = taper * jnp.cos(phase.astype(f32) * (2.0 * math.pi / WIN))
    table = lax.optimization_barrier(table).reshape(2, BINS, WIN)
    high = lax.reduce_precision(table, 8, 7)
    return jnp.concatenate([high.astype(bf16), (table - high).astype(bf16)], 1)


def scale_of(code):
    return jnp.exp2(code * (1.0 / STEPS)) * (1.0 / TOP)


def encode_kernel(samples, source, result, out, picked, extra, sems):
    step = pl.program_id(0)
    wide = samples.shape[2]
    blocks = wide // WIDTH
    steps = CHAN // blocks

    def copy(i):
        here = pl.ds(i * blocks, blocks)
        return pltpu.make_async_copy(
            out.at[here, :DATA, :], result.at[here, :DATA, :], sems.at[i]
        )

    @pl.when(step == 0)
    def _():
        picked[...] = jnp.zeros_like(picked)
        extra[...] = jnp.zeros_like(extra)

    number = lax.broadcasted_iota(jnp.int32, (wide, SOURCES), 0) + step * wide
    chooser = jnp.where(source[...] == number, 1.0, 0.0).astype(bf16)
    codes = []
    scales = []
    for w in range(KW):
        x = samples[w]
        peak = jnp.max(jnp.abs(x), axis=0, keepdims=True)
        scale = jnp.ceil(jnp.log2(jnp.maximum(peak, 1e-30)) * STEPS) + 1.0
        q = (x * (jnp.exp2(scale * (-1.0 / STEPS)) * TOP) + ROUND) - ROUND
        codes.append(q)
        scales.append(scale)
        qi = q.astype(jnp.int32).astype(jnp.int16)
        for k in range(blocks):
            out[step * blocks + k, w * SUB : (w + 1) * SUB, :] = qi[:, k * WIDTH : (k + 1) * WIDTH]
    copy(step).start()
    scales = jnp.concatenate(scales + [jnp.zeros((16 - KW, wide), f32)], 0)
    for k in range(blocks):
        for half in range(2):
            lane = k * WIDTH + half * 128
            start = pl.multiple_of((step * blocks + k) * 16 + 8, 8)
            extra[half, pl.ds(start, 8), :] = scales[:8, lane : lane + 128]
    high, low = split(jnp.concatenate(codes + [scales], 0))
    both = jnp.dot(jnp.concatenate([high, low], 0), chooser, preferred_element_type=f32)
    picked[:ROWS, :] += both[:ROWS] + both[ROWS:]

    @pl.when(step == pl.num_programs(0) - 1)
    def _():
        chosen = picked[...].T
        for half in range(2):
            part = chosen[:, half * 128 : half * 128 + 128]
            for d in range(NEAR):
                for z in range(2):
                    row = (d // 4 * 8 + z * 4 + d % 4) * 16
                    extra[half, row : row + PICK, :] = part[d * PICK : (d + 1) * PICK]
            rows = extra[half].reshape(CHAN, 16, 128)
            out[:, DATA:, half * 128 : half * 128 + 128] = rows.astype(jnp.int32).astype(jnp.int16)
        last = pltpu.make_async_copy(out.at[:, DATA:, :], result.at[:, DATA:, :], sems.at[steps])
        last.start()
        for i in range(steps):
            copy(i).wait()
        last.wait()


def encode(samples, source_index):
    wide = 2048
    steps = samples.shape[2] // wide
    return pl.pallas_call(
        encode_kernel,
        grid=(steps,),
        in_specs=[
            pl.BlockSpec((KW, SUB, wide), lambda i: (0, 0, i)),
            pl.BlockSpec((1, SOURCES), lambda i: (0, 0)),
        ],
        out_specs=pl.BlockSpec(memory_space=pl.ANY),
        out_shape=jax.ShapeDtypeStruct((CHAN, ROWS, WIDTH), jnp.int16),
        scratch_shapes=[
            pltpu.VMEM((CHAN, ROWS, WIDTH), jnp.int16),
            pltpu.VMEM((WIDTH, SOURCES), f32),
            pltpu.VMEM((2, CHAN * 16, 128), f32),
            pltpu.SemaphoreType.DMA((steps + 1,)),
        ],
        compiler_params=pltpu.CompilerParams(vmem_limit_bytes=VMEM),
        name="encode",
    )(samples, source_index.reshape(1, SOURCES))


def transform_kernel(mine, codes, extra, table, live, *rest):
    outs, (scale, white) = rest[:-2], rest[-2:]
    step = pl.program_id(0)
    rows = 2 * BAND
    batch = codes.shape[1] // SUB

    @pl.when(step == 0)
    def _():
        scale[...] = scale_of(extra[...].astype(jnp.int32).astype(f32)[:, 8:, :])

    for v in range(batch):
        value = codes[:, v * SUB : (v + 1) * SUB, :].astype(jnp.int32).astype(f32)
        value = value * scale[:, pl.ds(step * batch + v, 1), :]
        high, low = split(value.reshape(WIN, WIDTH))
        y = jnp.dot(table[0], high, preferred_element_type=f32)
        z = jnp.dot(table[0, : TM * rows], low, preferred_element_type=f32)
        for k in range(TM):
            part = slice(k * rows, (k + 1) * rows)
            value = y[part] + (y[(TM + k) * rows : (TM + k + 1) * rows] + z[part])
            power = jnp.sum(value * value, axis=0, keepdims=True) * (1.0 / BAND)
            white[k] = (value * (live[...] * lax.rsqrt(power + EPS))).astype(bf16)
        for k in range(TM):
            outs[k][v * rows : (v + 1) * rows, :] = white[jnp.bitwise_xor(mine[0], k)]


def transform(mine, received, table, live, band):
    rows = 2 * BAND
    batch = 2
    piece = pl.BlockSpec((batch * rows, WIDTH), lambda w, _: (w, 0))
    out_specs = [piece] * TM
    shapes = [jax.ShapeDtypeStruct((KW * rows, WIDTH), bf16)] * TM
    return pl.pallas_call(
        transform_kernel,
        grid_spec=pltpu.PrefetchScalarGridSpec(
            num_scalar_prefetch=1,
            grid=(KW // batch,),
            in_specs=[
                pl.BlockSpec((CHAN, batch * SUB, WIDTH), lambda w, _: (0, w, 0)),
                pl.BlockSpec((CHAN, 16, WIDTH), lambda w, _: (0, DATA // 16, 0)),
                pl.BlockSpec((1, 2 * BINS, WIN), lambda w, _: (band, 0, 0)),
                pl.BlockSpec((1, WIDTH), lambda w, _: (0, 0)),
            ],
            out_specs=out_specs,
            scratch_shapes=[pltpu.VMEM((CHAN, 8, WIDTH), f32), pltpu.VMEM((TM, rows, WIDTH), bf16)],
        ),
        out_shape=shapes,
        compiler_params=pltpu.CompilerParams(vmem_limit_bytes=VMEM),
        cost_estimate=LONG,
        name="transform",
    )(mine, received, received, table, live)


def sources_kernel(mine, extra, table, live, *rest):
    outs, (x, bands) = rest[:TM], rest[TM:]
    for first in range(0, CHAN, 4):
        values = [extra[d].astype(jnp.int32).astype(f32)[:PICK] for d in range(first, first + 4)]
        scales = [scale_of(value[:, DATA : DATA + KW]) for value in values]
        for w in range(KW):
            x[w * PICK : (w + 1) * PICK, first * SUB : (first + 4) * SUB] = jnp.concatenate(
                [
                    value[:, w * SUB : (w + 1) * SUB] * scale[:, w : w + 1]
                    for value, scale in zip(values, scales)
                ],
                1,
            )
    high, low = split(x[...])
    over = (((1,), (1,)), ((), ()))
    rows = 2 * BAND
    for b in range(2):
        y = lax.dot_general(high, table[b], over, preferred_element_type=f32)
        z = lax.dot_general(low, table[b, : TM * rows], over, preferred_element_type=f32)
        value = y[:, : TM * rows] + (y[:, TM * rows :] + z)
        for k in range(TM):
            band = value[:, k * rows : (k + 1) * rows]
            power = jnp.sum(band * band, axis=1, keepdims=True) * (1.0 / BAND)
            bands[b, k] = band * (live[...] * lax.rsqrt(power + EPS))
    for b in range(2):
        for k in range(TM):
            value = bands[b, jnp.bitwise_xor(mine[0], k)]
            outs[k][:, b * rows : (b + 1) * rows] = value.astype(bf16)


def sources(mine, received, table, live):
    rows = 2 * BAND
    piece = pl.BlockSpec((KW * PICK, WIDTH), lambda i: (0, 0))
    return pl.pallas_call(
        sources_kernel,
        grid=(1,),
        in_specs=[
            pl.BlockSpec(memory_space=pltpu.SMEM),
            pl.BlockSpec((CHAN, 16, WIDTH), lambda i: (0, DATA // 16, 0)),
            pl.BlockSpec((2, 2 * BINS, WIN), lambda i: (0, 0, 0)),
            pl.BlockSpec((KW * PICK, 1), lambda i: (0, 0)),
        ],
        out_specs=[piece] * TM,
        out_shape=[jax.ShapeDtypeStruct((KW * PICK, WIDTH), bf16)] * TM,
        scratch_shapes=[pltpu.VMEM((KW * PICK, WIN), f32), pltpu.VMEM((2, TM, KW * PICK, rows), f32)],
        compiler_params=pltpu.CompilerParams(vmem_limit_bytes=VMEM_LEAST),
        name="sources",
    )(mine, received, table, live)


def pack_kernel(a, b, c, d, out):
    parts = [u[...].astype(f32) for u in (a, b, c, d)]
    rows = [part[w * PICK : (w + 1) * PICK] for part in parts for w in range(KW)]
    block = lax.broadcasted_iota(jnp.int32, (PICK, 128), 1) // (2 * GROUP)
    for band in range(2):
        tiles = []
        pieces = [row[:, band * 128 : band * 128 + 128] for row in rows]
        for g in range(16):
            tile = jnp.zeros((PICK, 128), f32)
            for v in range(16):
                tile = jnp.where(block == v, pltpu.roll(pieces[v], (v - g) * 8 % 128, 1), tile)
            tiles.append(tile)
        for g in range(8):
            tile = jnp.zeros((PICK, 128), f32)
            for v in range(16):
                shift = (v - g * 2 - v // 8) * 8 % 128
                tile = jnp.where(block == v, pltpu.roll(pieces[16 + v % 8], shift, 1), tile)
            tiles.append(tile)
        value = jnp.concatenate(tiles, 0).astype(bf16)
        for d in range(NEAR):
            out[d, band] = value


def pack(spectra):
    whole = pl.BlockSpec(memory_space=pltpu.VMEM)
    return pl.pallas_call(
        pack_kernel,
        in_specs=[whole] * TM,
        out_specs=whole,
        out_shape=jax.ShapeDtypeStruct((NEAR, 2, 24 * PICK, 128), bf16),
        compiler_params=pltpu.CompilerParams(vmem_limit_bytes=VMEM_LESS),
        name="pack",
    )(*spectra)


def stack_kernel(band, sources, a, b, c, d, *rest):
    result, out, tiles, sems = rest[-4:]
    steps = BAND // GROUP // 2
    column = lax.broadcasted_iota(jnp.int32, (1, DEPTH), 1) % GROUP
    masks = [jnp.where(column == i, 1.0, 0.0).astype(bf16) for i in range(GROUP)]
    second = lax.broadcasted_iota(jnp.int32, (1, 128), 1) // GROUP % 2 == 1

    def copy(g):
        start = band * BAND + g * 2 * GROUP
        return pltpu.make_async_copy(
            out.at[pl.ds(g * 2 * GROUP, 2 * GROUP)],
            result.at[pl.ds(start, 2 * GROUP)],
            sems.at[g],
        )

    for place in range(NEAR):
        value = sources[place, 0].astype(f32).reshape(24, PICK, 128)
        tiles[:, place * PICK : (place + 1) * PICK, :] = value

    def imaginary(value):
        ahead = pltpu.roll(value, 128 - GROUP, 1)
        behind = pltpu.roll(value, GROUP, 1)
        return jnp.where(second, -behind, ahead)

    def body(g, carry):
        parts = [
            jnp.stack([u[pl.ds(pl.multiple_of(w * 2 * BAND + g * 16, 16), 16), :] for w in range(KW)])
            for u in (a, b, c, d)
        ]
        parts = [u.astype(f32) for u in parts]
        late = tiles[16 + g]
        for h in range(2):
            right = jnp.concatenate([u[:, h * 8 : h * 8 + 8, :] for u in parts], 0)
            right = right.reshape(DEPTH, WIDTH).astype(bf16)
            early = tiles[g * 2 + h]
            later = pltpu.roll(late, 64, 1) if h else late
            value = jnp.concatenate(
                [
                    jnp.concatenate([early, imaginary(early)], 0),
                    jnp.concatenate([later, imaginary(later)], 0)[:, :64],
                ],
                1,
            ).astype(bf16)
            for i in range(GROUP):
                product = jnp.dot(value * masks[i], right, preferred_element_type=f32)
                out[(g * 2 + h) * GROUP + i] = (
                    (product * (1.0 / WINDOWS)).reshape(2, SOURCES, WIDTH).astype(bf16)
                )
        copy(g).start()
        return carry

    lax.fori_loop(0, steps, body, 0, unroll=True)

    def finish(g, carry):
        copy(g).wait()
        return carry

    lax.fori_loop(0, steps, finish, 0)


def stack(sources, parts, band, before):
    whole = pl.BlockSpec((KW * 2 * BAND, WIDTH), lambda i: (0, 0))
    extra = [] if before is None else [before]
    return pl.pallas_call(
        functools.partial(stack_kernel, band),
        grid=(1,),
        in_specs=[pl.BlockSpec((NEAR, 1, 24 * PICK, 128), lambda i: (0, band, 0, 0))]
        + [whole] * TM
        + [pl.BlockSpec(memory_space=pl.ANY)] * len(extra),
        out_specs=pl.BlockSpec(memory_space=pl.ANY),
        out_shape=jax.ShapeDtypeStruct((BINS // TM, 2, SOURCES, WIDTH), bf16),
        scratch_shapes=[
            pltpu.VMEM((BAND, 2, SOURCES, WIDTH), bf16),
            pltpu.VMEM((24, SOURCES, 128), f32),
            pltpu.SemaphoreType.DMA((BAND // GROUP // 2,)),
        ],
        input_output_aliases={} if before is None else {1 + TM: 0},
        compiler_params=pltpu.CompilerParams(vmem_limit_bytes=VMEM_LESS),
        name="stack",
    )(sources, *parts, *extra)


def swap(value, axis, size, distance):
    return lax.ppermute(value, axis, [(i, i ^ distance) for i in range(size)])


def after(value, *others):
    return lax.optimization_barrier((value,) + others)[0]


def shards(samples, source_index, dead_flags):
    place = lax.axis_index("chan").astype(jnp.int32)
    mine = lax.axis_index("tm").astype(jnp.int32).reshape(1)
    live_all = 1.0 - dead_flags.astype(f32)
    live = lax.dynamic_slice_in_dim(live_all, place * WIDTH, WIDTH).reshape(1, WIDTH)
    place = place // 8 * 4 + place % 4
    own_sources = lax.dynamic_slice_in_dim(source_index, place * PICK, PICK)
    live_source = jnp.tile(live_all[own_sources], KW).reshape(KW * PICK, 1)
    table = dft_table()

    received = lax.all_to_all(encode(samples, source_index), "chan", 0, 0, tiled=True)
    spectra = sources(mine, received, table, live_source)
    spectra = [spectra[0]] + [swap(spectra[k], "tm", TM, k) for k in range(1, TM)]
    pieces = transform(mine, after(received, spectra[0]), table, live, 0)
    first = [pieces[0]] + [swap(after(pieces[k], *spectra[1:]), "tm", TM, k) for k in range(1, TM)]
    packed = pack([after(spectra[0], pieces[0])] + spectra[1:])
    groups = [[x * 8 + z * 4 + y for x in range(4) for y in range(4)] for z in range(2)]
    left = lax.all_to_all(packed, "chan", 0, 0, tiled=True, axis_index_groups=groups)
    pieces = transform(mine, after(received, packed), table, live, 1)
    second = [pieces[0]] + [
        swap(pieces[k], "tm", TM, k) for k in range(1, TM)
    ]
    result = stack(left, first, 0, None)
    return stack(left, second, 1, result)


def solution(mesh):
    return jax.shard_map(
        shards,
        mesh=mesh,
        in_specs=(P("tm", "chan", None), P(), P()),
        out_specs=P("tm", None, None, "chan"),
        check_vma=False,
    )
```

```python
import functools
import math

import jax
import jax.numpy as jnp
from jax import lax
from jax.experimental import pallas as pl
from jax.experimental.pallas import tpu as pltpu
from jax.sharding import PartitionSpec as P

WIN = 1024
BINS = 512
BAND = 64
WINDOWS = 24
SOURCES = 128
CHAN = 32
TM = 4
KW = WINDOWS // TM
SUB = WIN // CHAN
WIDTH = 256
NEAR = 16
PICK = SOURCES // NEAR
DATA = KW * SUB
ROWS = DATA + 16
GROUP = 4
DEPTH = WINDOWS * 2 * GROUP
STEPS = 128.0
TOP = 32767.0
ROUND = 1.5 * 2.0**23
EPS = 1e-06
VMEM = 56 * 1024 * 1024
VMEM_LESS = 46 * 1024 * 1024
VMEM_MID = 50 * 1024 * 1024
LONG = pl.CostEstimate(flops=40 * 10**9, bytes_accessed=10**8, transcendentals=0)

f32 = jnp.float32
bf16 = jnp.bfloat16


def split(x):
    high = x.astype(bf16)
    return high, (x - high.astype(f32)).astype(bf16)


def dft_table():
    row = jnp.arange(2 * BINS, dtype=jnp.int32)[:, None]
    sample = jnp.arange(WIN, dtype=jnp.int32)[None, :]
    rows = 2 * BAND
    place = row // (TM * rows) * BAND + row // rows % TM * (2 * BAND)
    frequency = place + row % rows // (2 * GROUP) * GROUP + row % GROUP
    part = row // GROUP % 2
    phase = jnp.bitwise_and(sample * frequency + part * (WIN // 4), WIN - 1)
    turn = WIN // 4 - jnp.abs(phase - WIN // 2)
    angle = turn.astype(f32) * (2.0 * math.pi / WIN)
    square = angle * angle
    series = jnp.full_like(square, -1.0 / math.factorial(11))
    for power in (9, 7, 5, 3, 1):
        series = series * square + (-1.0) ** (power // 2) / math.factorial(power)
    taper = 0.5 - 0.5 * jnp.cos((sample.astype(f32) + 0.5) * (2.0 * math.pi / WIN))
    table = taper * (-angle * series)
    table = lax.optimization_barrier(table).reshape(2, BINS, WIN)
    high = lax.reduce_precision(table, 8, 7)
    return jnp.concatenate([high.astype(bf16), (table - high).astype(bf16)], 1)


def scale_of(code):
    return jnp.exp2(code * (1.0 / STEPS)) * (1.0 / TOP)


def encode_kernel(samples, source, result, out, picked, extra, sems):
    step = pl.program_id(0)
    wide = samples.shape[2]
    blocks = wide // WIDTH
    steps = CHAN // blocks

    def copy(i):
        here = pl.ds(i * blocks, blocks)
        return pltpu.make_async_copy(
            out.at[here, :DATA, :], result.at[here, :DATA, :], sems.at[i]
        )

    @pl.when(step == 0)
    def _():
        picked[...] = jnp.zeros_like(picked)
        extra[...] = jnp.zeros_like(extra)

    number = lax.broadcasted_iota(jnp.int32, (wide, SOURCES), 0) + step * wide
    chooser = jnp.where(source[...] == number, 1.0, 0.0).astype(bf16)
    codes = []
    scales = []
    for w in range(KW):
        x = samples[w]
        peak = jnp.max(jnp.abs(x), axis=0, keepdims=True)
        scale = jnp.ceil(jnp.log2(jnp.maximum(peak, 1e-30)) * STEPS) + 1.0
        q = (x * (jnp.exp2(scale * (-1.0 / STEPS)) * TOP) + ROUND) - ROUND
        codes.append(q)
        scales.append(scale)
        qi = q.astype(jnp.int32).astype(jnp.int16)
        for k in range(blocks):
            out[step * blocks + k, w * SUB : (w + 1) * SUB, :] = qi[:, k * WIDTH : (k + 1) * WIDTH]
    copy(step).start()
    scales = jnp.concatenate(scales + [jnp.zeros((16 - KW, wide), f32)], 0)
    for k in range(blocks):
        for half in range(2):
            lane = k * WIDTH + half * 128
            start = pl.multiple_of((step * blocks + k) * 16 + 8, 8)
            extra[half, pl.ds(start, 8), :] = scales[:8, lane : lane + 128]
    high, low = split(jnp.concatenate(codes + [scales], 0))
    both = jnp.dot(jnp.concatenate([high, low], 0), chooser, preferred_element_type=f32)
    picked[:ROWS, :] += both[:ROWS] + both[ROWS:]

    @pl.when(step == pl.num_programs(0) - 1)
    def _():
        chosen = picked[...].T
        for half in range(2):
            part = chosen[:, half * 128 : half * 128 + 128]
            for d in range(NEAR):
                for z in range(2):
                    row = (d // 4 * 8 + z * 4 + d % 4) * 16
                    extra[half, row : row + PICK, :] = part[d * PICK : (d + 1) * PICK]
            rows = extra[half].reshape(CHAN, 16, 128)
            out[:, DATA:, half * 128 : half * 128 + 128] = rows.astype(jnp.int32).astype(jnp.int16)
        last = pltpu.make_async_copy(out.at[:, DATA:, :], result.at[:, DATA:, :], sems.at[steps])
        last.start()
        for i in range(steps):
            copy(i).wait()
        last.wait()


def encode(samples, source_index):
    wide = 2048
    steps = samples.shape[2] // wide
    return pl.pallas_call(
        encode_kernel,
        grid=(steps,),
        in_specs=[
            pl.BlockSpec((KW, SUB, wide), lambda i: (0, 0, i)),
            pl.BlockSpec((1, SOURCES), lambda i: (0, 0)),
        ],
        out_specs=pl.BlockSpec(memory_space=pl.ANY),
        out_shape=jax.ShapeDtypeStruct((CHAN, ROWS, WIDTH), jnp.int16),
        scratch_shapes=[
            pltpu.VMEM((CHAN, ROWS, WIDTH), jnp.int16),
            pltpu.VMEM((WIDTH, SOURCES), f32),
            pltpu.VMEM((2, CHAN * 16, 128), f32),
            pltpu.SemaphoreType.DMA((steps + 1,)),
        ],
        compiler_params=pltpu.CompilerParams(vmem_limit_bytes=VMEM),
        name="encode",
    )(samples, source_index.reshape(1, SOURCES))


def transform_kernel(mine, codes, extra, table, live, *rest):
    both = len(rest) > TM + 2
    if both:
        live_source, rest = rest[0], rest[1:]
        spectra, (x, bands), rest = rest[TM : 2 * TM], rest[-2:], rest[:TM] + rest[2 * TM : -2]
    outs, (scale, white) = rest[:-2], rest[-2:]
    step = pl.program_id(0)
    rows = 2 * BAND
    batch = codes.shape[1] // SUB

    @pl.when(step == 0)
    def _():
        if both:
            transform_sources(mine, extra, table, live_source, spectra, x, bands)
        scale[...] = scale_of(extra[...].astype(jnp.int32).astype(f32)[:, 8:, :])

    for v in range(batch):
        value = codes[:, v * SUB : (v + 1) * SUB, :].astype(jnp.int32).astype(f32)
        value = value * scale[:, pl.ds(step * batch + v, 1), :]
        high, low = split(value.reshape(WIN, WIDTH))
        y = jnp.dot(table[0], high, preferred_element_type=f32)
        z = jnp.dot(table[0, : TM * rows], low, preferred_element_type=f32)
        for k in range(TM):
            part = slice(k * rows, (k + 1) * rows)
            value = y[part] + (y[(TM + k) * rows : (TM + k + 1) * rows] + z[part])
            power = jnp.sum(value * value, axis=0, keepdims=True) * (1.0 / BAND)
            white[k] = (value * (live[...] * lax.rsqrt(power + EPS))).astype(bf16)
        for k in range(TM):
            outs[k][v * rows : (v + 1) * rows, :] = white[jnp.bitwise_xor(mine[0], k)]


def transform(mine, received, table, live, band, live_source=None):
    rows = 2 * BAND
    batch = 2
    both = live_source is not None
    in_specs = [
        pl.BlockSpec((CHAN, batch * SUB, WIDTH), lambda w, _: (0, w, 0)),
        pl.BlockSpec((CHAN, 16, WIDTH), lambda w, _: (0, DATA // 16, 0)),
        pl.BlockSpec((2 if both else 1, 2 * BINS, WIN), lambda w, _: (band, 0, 0)),
        pl.BlockSpec((1, WIDTH), lambda w, _: (0, 0)),
    ]
    inputs = [received, received, table, live]
    out_specs = [pl.BlockSpec((batch * rows, WIDTH), lambda w, _: (w, 0))] * TM
    shapes = [jax.ShapeDtypeStruct((KW * rows, WIDTH), bf16)] * TM
    scratch = [pltpu.VMEM((CHAN, 8, WIDTH), f32), pltpu.VMEM((TM, rows, WIDTH), bf16)]
    if both:
        in_specs += [pl.BlockSpec((KW * PICK, 1), lambda w, _: (0, 0))]
        inputs += [live_source]
        out_specs += [pl.BlockSpec((KW * PICK, 2 * rows), lambda w, _: (0, 0))] * TM
        shapes += [jax.ShapeDtypeStruct((KW * PICK, 2 * rows), bf16)] * TM
        scratch += [pltpu.VMEM((KW * PICK, WIN), f32), pltpu.VMEM((2, TM, KW * PICK, rows), f32)]
    outs = pl.pallas_call(
        transform_kernel,
        grid_spec=pltpu.PrefetchScalarGridSpec(
            num_scalar_prefetch=1,
            grid=(KW // batch,),
            in_specs=in_specs,
            out_specs=out_specs,
            scratch_shapes=scratch,
        ),
        out_shape=shapes,
        compiler_params=pltpu.CompilerParams(vmem_limit_bytes=VMEM_MID if both else VMEM),
        cost_estimate=LONG,
        name="transform",
    )(mine, *inputs)
    return outs[:TM], outs[TM:]


def transform_sources(mine, extra, table, live, outs, x, bands):
    for first in range(0, CHAN, 4):
        values = [extra[d].astype(jnp.int32).astype(f32)[:PICK] for d in range(first, first + 4)]
        scales = [scale_of(value[:, DATA : DATA + KW]) for value in values]
        for w in range(KW):
            x[w * PICK : (w + 1) * PICK, first * SUB : (first + 4) * SUB] = jnp.concatenate(
                [
                    value[:, w * SUB : (w + 1) * SUB] * scale[:, w : w + 1]
                    for value, scale in zip(values, scales)
                ],
                1,
            )
    high, low = split(x[...])
    over = (((1,), (1,)), ((), ()))
    rows = 2 * BAND
    for b in range(2):
        y = lax.dot_general(high, table[b], over, preferred_element_type=f32)
        z = lax.dot_general(low, table[b, : TM * rows], over, preferred_element_type=f32)
        value = y[:, : TM * rows] + (y[:, TM * rows :] + z)
        for k in range(TM):
            band = value[:, k * rows : (k + 1) * rows]
            power = jnp.sum(band * band, axis=1, keepdims=True) * (1.0 / BAND)
            bands[b, k] = band * (live[...] * lax.rsqrt(power + EPS))
    for b in range(2):
        for k in range(TM):
            value = bands[b, jnp.bitwise_xor(mine[0], k)]
            outs[k][:, b * rows : (b + 1) * rows] = value.astype(bf16)


def pack_kernel(a, b, c, d, out):
    parts = [u[...].astype(f32) for u in (a, b, c, d)]
    rows = [part[w * PICK : (w + 1) * PICK] for part in parts for w in range(KW)]
    block = lax.broadcasted_iota(jnp.int32, (PICK, 128), 1) // (2 * GROUP)
    for band in range(2):
        tiles = []
        pieces = [row[:, band * 128 : band * 128 + 128] for row in rows]
        for g in range(16):
            tile = jnp.zeros((PICK, 128), f32)
            for v in range(16):
                tile = jnp.where(block == v, pltpu.roll(pieces[v], (v - g) * 8 % 128, 1), tile)
            tiles.append(tile)
        for g in range(8):
            tile = jnp.zeros((PICK, 128), f32)
            for v in range(16):
                shift = (v - g * 2 - v // 8) * 8 % 128
                tile = jnp.where(block == v, pltpu.roll(pieces[16 + v % 8], shift, 1), tile)
            tiles.append(tile)
        value = jnp.concatenate(tiles, 0).astype(bf16)
        for d in range(NEAR):
            out[d, band] = value


def pack(spectra):
    whole = pl.BlockSpec(memory_space=pltpu.VMEM)
    return pl.pallas_call(
        pack_kernel,
        in_specs=[whole] * TM,
        out_specs=whole,
        out_shape=jax.ShapeDtypeStruct((NEAR, 2, 24 * PICK, 128), bf16),
        compiler_params=pltpu.CompilerParams(vmem_limit_bytes=VMEM_LESS),
        name="pack",
    )(*spectra)


def stack_kernel(band, sources, a, b, c, d, *rest):
    result, out, tiles, sems = rest[-4:]
    steps = BAND // GROUP // 2
    column = lax.broadcasted_iota(jnp.int32, (1, DEPTH), 1) % GROUP
    masks = [jnp.where(column == i, 1.0, 0.0).astype(bf16) for i in range(GROUP)]
    second = lax.broadcasted_iota(jnp.int32, (1, 128), 1) // GROUP % 2 == 1

    def copy(g):
        start = band * BAND + g * 2 * GROUP
        return pltpu.make_async_copy(
            out.at[pl.ds(g * 2 * GROUP, 2 * GROUP)],
            result.at[pl.ds(start, 2 * GROUP)],
            sems.at[g],
        )

    for place in range(NEAR):
        value = sources[place, 0].astype(f32).reshape(24, PICK, 128)
        tiles[:, place * PICK : (place + 1) * PICK, :] = value

    def imaginary(value):
        ahead = pltpu.roll(value, 128 - GROUP, 1)
        behind = pltpu.roll(value, GROUP, 1)
        return jnp.where(second, -behind, ahead)

    def body(g, carry):
        parts = [
            jnp.stack([u[pl.ds(pl.multiple_of(w * 2 * BAND + g * 16, 16), 16), :] for w in range(KW)])
            for u in (a, b, c, d)
        ]
        parts = [u.astype(f32) for u in parts]
        late = tiles[16 + g]
        for h in range(2):
            right = jnp.concatenate([u[:, h * 8 : h * 8 + 8, :] for u in parts], 0)
            right = right.reshape(DEPTH, WIDTH).astype(bf16)
            early = tiles[g * 2 + h]
            later = pltpu.roll(late, 64, 1) if h else late
            value = jnp.concatenate(
                [
                    jnp.concatenate([early, imaginary(early)], 0),
                    jnp.concatenate([later, imaginary(later)], 0)[:, :64],
                ],
                1,
            ).astype(bf16)
            for i in range(GROUP):
                product = jnp.dot(value * masks[i], right, preferred_element_type=f32)
                out[(g * 2 + h) * GROUP + i] = (
                    (product * (1.0 / WINDOWS)).reshape(2, SOURCES, WIDTH).astype(bf16)
                )
        copy(g).start()
        return carry

    lax.fori_loop(0, steps, body, 0, unroll=True)

    def finish(g, carry):
        copy(g).wait()
        return carry

    lax.fori_loop(0, steps, finish, 0)


def stack(sources, parts, band, before):
    whole = pl.BlockSpec((KW * 2 * BAND, WIDTH), lambda i: (0, 0))
    extra = [] if before is None else [before]
    return pl.pallas_call(
        functools.partial(stack_kernel, band),
        grid=(1,),
        in_specs=[pl.BlockSpec((NEAR, 1, 24 * PICK, 128), lambda i: (0, band, 0, 0))]
        + [whole] * TM
        + [pl.BlockSpec(memory_space=pl.ANY)] * len(extra),
        out_specs=pl.BlockSpec(memory_space=pl.ANY),
        out_shape=jax.ShapeDtypeStruct((BINS // TM, 2, SOURCES, WIDTH), bf16),
        scratch_shapes=[
            pltpu.VMEM((BAND, 2, SOURCES, WIDTH), bf16),
            pltpu.VMEM((24, SOURCES, 128), f32),
            pltpu.SemaphoreType.DMA((BAND // GROUP // 2,)),
        ],
        input_output_aliases={} if before is None else {1 + TM: 0},
        compiler_params=pltpu.CompilerParams(vmem_limit_bytes=VMEM_LESS),
        name="stack",
    )(sources, *parts, *extra)


def swap(value, axis, size, distance):
    return lax.ppermute(value, axis, [(i, i ^ distance) for i in range(size)])


def after(value, *others):
    return lax.optimization_barrier((value,) + others)[0]


def shards(samples, source_index, dead_flags):
    place = lax.axis_index("chan").astype(jnp.int32)
    mine = lax.axis_index("tm").astype(jnp.int32).reshape(1)
    live_all = 1.0 - dead_flags.astype(f32)
    live = lax.dynamic_slice_in_dim(live_all, place * WIDTH, WIDTH).reshape(1, WIDTH)
    place = place // 8 * 4 + place % 4
    own_sources = lax.dynamic_slice_in_dim(source_index, place * PICK, PICK)
    live_source = jnp.tile(live_all[own_sources], KW).reshape(KW * PICK, 1)
    table = dft_table()

    received = lax.all_to_all(encode(samples, source_index), "chan", 0, 0, tiled=True)
    pieces, spectra = transform(mine, received, table, live, 0, live_source)
    spectra = [spectra[0]] + [swap(spectra[k], "tm", TM, k) for k in range(1, TM)]
    first = [pieces[0]] + [swap(after(pieces[k], spectra[1]), "tm", TM, k) for k in range(1, TM)]
    packed = pack(spectra)
    groups = [[x * 8 + z * 4 + y for x in range(4) for y in range(4)] for z in range(2)]
    left = lax.all_to_all(packed, "chan", 0, 0, tiled=True, axis_index_groups=groups)
    pieces, _ = transform(mine, after(received, packed), table, live, 1)
    second = [pieces[0]] + [
        swap(pieces[k], "tm", TM, k) for k in range(1, TM)
    ]
    result = stack(left, first, 0, None)
    return stack(left, second, 1, result)


def solution(mesh):
    return jax.shard_map(
        shards,
        mesh=mesh,
        in_specs=(P("tm", "chan", None), P(), P()),
        out_specs=P("tm", None, None, "chan"),
        check_vma=False,
    )
```

```python
import functools
import math

import jax
import jax.numpy as jnp
from jax import lax
from jax.experimental import pallas as pl
from jax.experimental.pallas import tpu as pltpu
from jax.sharding import PartitionSpec as P

WIN = 1024
BINS = 512
BAND = 64
WINDOWS = 24
SOURCES = 128
CHAN = 32
TM = 4
KW = WINDOWS // TM
SUB = WIN // CHAN
WIDTH = 256
NEAR = 16
PICK = SOURCES // NEAR
DATA = KW * SUB
ROWS = DATA + 16
GROUP = 4
DEPTH = WINDOWS * 2 * GROUP
STEPS = 128.0
TOP = 32767.0
ROUND = 1.5 * 2.0**23
EPS = 1e-06
VMEM = 56 * 1024 * 1024
VMEM_LESS = 46 * 1024 * 1024
VMEM_MID = 50 * 1024 * 1024
LONG = pl.CostEstimate(flops=40 * 10**9, bytes_accessed=10**8, transcendentals=0)

f32 = jnp.float32
bf16 = jnp.bfloat16


def split(x):
    high = x.astype(bf16)
    return high, (x - high.astype(f32)).astype(bf16)


def dft_table():
    row = jnp.arange(2 * BINS, dtype=jnp.int32)[:, None]
    sample = jnp.arange(WIN, dtype=jnp.int32)[None, :]
    rows = 2 * BAND
    place = row // (TM * rows) * BAND + row // rows % TM * (2 * BAND)
    frequency = place + row % rows // (2 * GROUP) * GROUP + row % GROUP
    part = row // GROUP % 2
    phase = jnp.bitwise_and(sample * frequency + part * (WIN // 4), WIN - 1)
    turn = WIN // 4 - jnp.abs(phase - WIN // 2)
    angle = turn.astype(f32) * (2.0 * math.pi / WIN)
    square = angle * angle
    series = jnp.full_like(square, -1.0 / math.factorial(11))
    for power in (9, 7, 5, 3, 1):
        series = series * square + (-1.0) ** (power // 2) / math.factorial(power)
    taper = 0.5 - 0.5 * jnp.cos((sample.astype(f32) + 0.5) * (2.0 * math.pi / WIN))
    table = taper * (-angle * series)
    table = lax.optimization_barrier(table).reshape(2, BINS, WIN)
    high = lax.reduce_precision(table, 8, 7)
    return jnp.concatenate([high.astype(bf16), (table - high).astype(bf16)], 1)


def scale_of(code):
    return jnp.exp2(code * (1.0 / STEPS)) * (1.0 / TOP)


def encode_kernel(samples, source, result, out, picked, extra, sems):
    step = pl.program_id(0)
    wide = samples.shape[2]
    blocks = wide // WIDTH
    steps = CHAN // blocks

    def copy(i):
        here = pl.ds(i * blocks, blocks)
        return pltpu.make_async_copy(
            out.at[here, :DATA, :], result.at[here, :DATA, :], sems.at[i]
        )

    @pl.when(step == 0)
    def _():
        picked[...] = jnp.zeros_like(picked)
        extra[...] = jnp.zeros_like(extra)

    number = lax.broadcasted_iota(jnp.int32, (wide, SOURCES), 0) + step * wide
    chooser = jnp.where(source[...] == number, 1.0, 0.0).astype(bf16)
    codes = []
    scales = []
    for w in range(KW):
        x = samples[w]
        peak = jnp.max(jnp.abs(x), axis=0, keepdims=True)
        scale = jnp.ceil(jnp.log2(jnp.maximum(peak, 1e-30)) * STEPS) + 1.0
        q = (x * (jnp.exp2(scale * (-1.0 / STEPS)) * TOP) + ROUND) - ROUND
        codes.append(q)
        scales.append(scale)
        qi = q.astype(jnp.int32).astype(jnp.int16)
        for k in range(blocks):
            out[step * blocks + k, w * SUB : (w + 1) * SUB, :] = qi[:, k * WIDTH : (k + 1) * WIDTH]
    copy(step).start()
    scales = jnp.concatenate(scales + [jnp.zeros((16 - KW, wide), f32)], 0)
    for k in range(blocks):
        for half in range(2):
            lane = k * WIDTH + half * 128
            start = pl.multiple_of((step * blocks + k) * 16 + 8, 8)
            extra[half, pl.ds(start, 8), :] = scales[:8, lane : lane + 128]
    high, low = split(jnp.concatenate(codes + [scales], 0))
    both = jnp.dot(jnp.concatenate([high, low], 0), chooser, preferred_element_type=f32)
    picked[:ROWS, :] += both[:ROWS] + both[ROWS:]

    @pl.when(step == pl.num_programs(0) - 1)
    def _():
        chosen = picked[...].T
        for half in range(2):
            part = chosen[:, half * 128 : half * 128 + 128]
            for d in range(NEAR):
                for z in range(2):
                    row = (d // 4 * 8 + z * 4 + d % 4) * 16
                    extra[half, row : row + PICK, :] = part[d * PICK : (d + 1) * PICK]
            rows = extra[half].reshape(CHAN, 16, 128)
            out[:, DATA:, half * 128 : half * 128 + 128] = rows.astype(jnp.int32).astype(jnp.int16)
        last = pltpu.make_async_copy(out.at[:, DATA:, :], result.at[:, DATA:, :], sems.at[steps])
        last.start()
        for i in range(steps):
            copy(i).wait()
        last.wait()


def encode(samples, source_index):
    wide = 4096
    steps = samples.shape[2] // wide
    return pl.pallas_call(
        encode_kernel,
        grid=(steps,),
        in_specs=[
            pl.BlockSpec((KW, SUB, wide), lambda i: (0, 0, i)),
            pl.BlockSpec((1, SOURCES), lambda i: (0, 0)),
        ],
        out_specs=pl.BlockSpec(memory_space=pl.ANY),
        out_shape=jax.ShapeDtypeStruct((CHAN, ROWS, WIDTH), jnp.int16),
        scratch_shapes=[
            pltpu.VMEM((CHAN, ROWS, WIDTH), jnp.int16),
            pltpu.VMEM((WIDTH, SOURCES), f32),
            pltpu.VMEM((2, CHAN * 16, 128), f32),
            pltpu.SemaphoreType.DMA((steps + 1,)),
        ],
        compiler_params=pltpu.CompilerParams(vmem_limit_bytes=VMEM),
        name="encode",
    )(samples, source_index.reshape(1, SOURCES))


def transform_kernel(mine, codes, extra, table, live, *rest):
    both = len(rest) > TM + 2
    if both:
        live_source, rest = rest[0], rest[1:]
        spectra, (x, bands), rest = rest[TM : 2 * TM], rest[-2:], rest[:TM] + rest[2 * TM : -2]
    outs, (scale, white) = rest[:-2], rest[-2:]
    step = pl.program_id(0)
    rows = 2 * BAND
    batch = codes.shape[1] // SUB

    @pl.when(step == 0)
    def _():
        if both:
            transform_sources(mine, extra, table, live_source, spectra, x, bands)
        scale[...] = scale_of(extra[...].astype(jnp.int32).astype(f32)[:, 8:, :])

    for v in range(batch):
        value = codes[:, v * SUB : (v + 1) * SUB, :].astype(jnp.int32).astype(f32)
        value = value * scale[:, pl.ds(step * batch + v, 1), :]
        high, low = split(value.reshape(WIN, WIDTH))
        y = jnp.dot(table[0], high, preferred_element_type=f32)
        z = jnp.dot(table[0, : TM * rows], low, preferred_element_type=f32)
        for k in range(TM):
            part = slice(k * rows, (k + 1) * rows)
            value = y[part] + (y[(TM + k) * rows : (TM + k + 1) * rows] + z[part])
            power = jnp.sum(value * value, axis=0, keepdims=True) * (1.0 / BAND)
            white[k] = (value * (live[...] * lax.rsqrt(power + EPS))).astype(bf16)
        for k in range(TM):
            outs[k][v * rows : (v + 1) * rows, :] = white[jnp.bitwise_xor(mine[0], k)]


def transform(mine, received, table, live, band, live_source=None):
    rows = 2 * BAND
    batch = 2
    both = live_source is not None
    in_specs = [
        pl.BlockSpec((CHAN, batch * SUB, WIDTH), lambda w, _: (0, w, 0)),
        pl.BlockSpec((CHAN, 16, WIDTH), lambda w, _: (0, DATA // 16, 0)),
        pl.BlockSpec((2 if both else 1, 2 * BINS, WIN), lambda w, _: (band, 0, 0)),
        pl.BlockSpec((1, WIDTH), lambda w, _: (0, 0)),
    ]
    inputs = [received, received, table, live]
    out_specs = [pl.BlockSpec((batch * rows, WIDTH), lambda w, _: (w, 0))] * TM
    shapes = [jax.ShapeDtypeStruct((KW * rows, WIDTH), bf16)] * TM
    scratch = [pltpu.VMEM((CHAN, 8, WIDTH), f32), pltpu.VMEM((TM, rows, WIDTH), bf16)]
    if both:
        in_specs += [pl.BlockSpec((KW * PICK, 1), lambda w, _: (0, 0))]
        inputs += [live_source]
        out_specs += [pl.BlockSpec((KW * PICK, 2 * rows), lambda w, _: (0, 0))] * TM
        shapes += [jax.ShapeDtypeStruct((KW * PICK, 2 * rows), bf16)] * TM
        scratch += [pltpu.VMEM((KW * PICK, WIN), f32), pltpu.VMEM((2, TM, KW * PICK, rows), f32)]
    outs = pl.pallas_call(
        transform_kernel,
        grid_spec=pltpu.PrefetchScalarGridSpec(
            num_scalar_prefetch=1,
            grid=(KW // batch,),
            in_specs=in_specs,
            out_specs=out_specs,
            scratch_shapes=scratch,
        ),
        out_shape=shapes,
        compiler_params=pltpu.CompilerParams(vmem_limit_bytes=VMEM_MID if both else VMEM),
        cost_estimate=LONG,
        name="transform",
    )(mine, *inputs)
    return outs[:TM], outs[TM:]


def transform_sources(mine, extra, table, live, outs, x, bands):
    for first in range(0, CHAN, 4):
        values = [extra[d].astype(jnp.int32).astype(f32)[:PICK] for d in range(first, first + 4)]
        scales = [scale_of(value[:, DATA : DATA + KW]) for value in values]
        for w in range(KW):
            x[w * PICK : (w + 1) * PICK, first * SUB : (first + 4) * SUB] = jnp.concatenate(
                [
                    value[:, w * SUB : (w + 1) * SUB] * scale[:, w : w + 1]
                    for value, scale in zip(values, scales)
                ],
                1,
            )
    high, low = split(x[...])
    over = (((1,), (1,)), ((), ()))
    rows = 2 * BAND
    for b in range(2):
        y = lax.dot_general(high, table[b], over, preferred_element_type=f32)
        z = lax.dot_general(low, table[b, : TM * rows], over, preferred_element_type=f32)
        value = y[:, : TM * rows] + (y[:, TM * rows :] + z)
        for k in range(TM):
            band = value[:, k * rows : (k + 1) * rows]
            power = jnp.sum(band * band, axis=1, keepdims=True) * (1.0 / BAND)
            bands[b, k] = band * (live[...] * lax.rsqrt(power + EPS))
    for b in range(2):
        for k in range(TM):
            value = bands[b, jnp.bitwise_xor(mine[0], k)]
            outs[k][:, b * rows : (b + 1) * rows] = value.astype(bf16)


def pack_kernel(a, b, c, d, out):
    parts = [u[...].astype(f32) for u in (a, b, c, d)]
    rows = [part[w * PICK : (w + 1) * PICK] for part in parts for w in range(KW)]
    block = lax.broadcasted_iota(jnp.int32, (PICK, 128), 1) // (2 * GROUP)
    for band in range(2):
        tiles = []
        pieces = [row[:, band * 128 : band * 128 + 128] for row in rows]
        for g in range(16):
            tile = jnp.zeros((PICK, 128), f32)
            for v in range(16):
                tile = jnp.where(block == v, pltpu.roll(pieces[v], (v - g) * 8 % 128, 1), tile)
            tiles.append(tile)
        for g in range(8):
            tile = jnp.zeros((PICK, 128), f32)
            for v in range(16):
                shift = (v - g * 2 - v // 8) * 8 % 128
                tile = jnp.where(block == v, pltpu.roll(pieces[16 + v % 8], shift, 1), tile)
            tiles.append(tile)
        value = jnp.concatenate(tiles, 0).astype(bf16)
        for d in range(NEAR):
            out[d, band] = value


def pack(spectra):
    whole = pl.BlockSpec(memory_space=pltpu.VMEM)
    return pl.pallas_call(
        pack_kernel,
        in_specs=[whole] * TM,
        out_specs=whole,
        out_shape=jax.ShapeDtypeStruct((NEAR, 2, 24 * PICK, 128), bf16),
        compiler_params=pltpu.CompilerParams(vmem_limit_bytes=VMEM_LESS),
        name="pack",
    )(*spectra)


def stack_kernel(band, sources, a, b, c, d, *rest):
    result, out, tiles, sems = rest[-4:]
    steps = BAND // GROUP // 2
    column = lax.broadcasted_iota(jnp.int32, (1, DEPTH), 1) % GROUP
    masks = [jnp.where(column == i, 1.0, 0.0).astype(bf16) for i in range(GROUP)]
    second = lax.broadcasted_iota(jnp.int32, (1, 128), 1) // GROUP % 2 == 1

    def copy(g):
        start = band * BAND + g * 2 * GROUP
        return pltpu.make_async_copy(
            out.at[pl.ds(g * 2 * GROUP, 2 * GROUP)],
            result.at[pl.ds(start, 2 * GROUP)],
            sems.at[g],
        )

    for place in range(NEAR):
        value = sources[place, 0].astype(f32).reshape(24, PICK, 128)
        tiles[:, place * PICK : (place + 1) * PICK, :] = value

    def imaginary(value):
        ahead = pltpu.roll(value, 128 - GROUP, 1)
        behind = pltpu.roll(value, GROUP, 1)
        return jnp.where(second, -behind, ahead)

    def body(g, carry):
        parts = [
            jnp.stack([u[pl.ds(pl.multiple_of(w * 2 * BAND + g * 16, 16), 16), :] for w in range(KW)])
            for u in (a, b, c, d)
        ]
        parts = [u.astype(f32) for u in parts]
        late = tiles[16 + g]
        for h in range(2):
            right = jnp.concatenate([u[:, h * 8 : h * 8 + 8, :] for u in parts], 0)
            right = right.reshape(DEPTH, WIDTH).astype(bf16)
            early = tiles[g * 2 + h]
            later = pltpu.roll(late, 64, 1) if h else late
            value = jnp.concatenate(
                [
                    jnp.concatenate([early, imaginary(early)], 0),
                    jnp.concatenate([later, imaginary(later)], 0)[:, :64],
                ],
                1,
            ).astype(bf16)
            for i in range(GROUP):
                product = jnp.dot(value * masks[i], right, preferred_element_type=f32)
                out[(g * 2 + h) * GROUP + i] = (
                    (product * (1.0 / WINDOWS)).reshape(2, SOURCES, WIDTH).astype(bf16)
                )
        copy(g).start()
        return carry

    lax.fori_loop(0, steps, body, 0, unroll=True)

    def finish(g, carry):
        copy(g).wait()
        return carry

    lax.fori_loop(0, steps, finish, 0)


def stack(sources, parts, band, before):
    whole = pl.BlockSpec((KW * 2 * BAND, WIDTH), lambda i: (0, 0))
    extra = [] if before is None else [before]
    return pl.pallas_call(
        functools.partial(stack_kernel, band),
        grid=(1,),
        in_specs=[pl.BlockSpec((NEAR, 1, 24 * PICK, 128), lambda i: (0, band, 0, 0))]
        + [whole] * TM
        + [pl.BlockSpec(memory_space=pl.ANY)] * len(extra),
        out_specs=pl.BlockSpec(memory_space=pl.ANY),
        out_shape=jax.ShapeDtypeStruct((BINS // TM, 2, SOURCES, WIDTH), bf16),
        scratch_shapes=[
            pltpu.VMEM((BAND, 2, SOURCES, WIDTH), bf16),
            pltpu.VMEM((24, SOURCES, 128), f32),
            pltpu.SemaphoreType.DMA((BAND // GROUP // 2,)),
        ],
        input_output_aliases={} if before is None else {1 + TM: 0},
        compiler_params=pltpu.CompilerParams(vmem_limit_bytes=VMEM_LESS),
        name="stack",
    )(sources, *parts, *extra)


def swap(value, axis, size, distance):
    return lax.ppermute(value, axis, [(i, i ^ distance) for i in range(size)])


def after(value, *others):
    return lax.optimization_barrier((value,) + others)[0]


def shards(samples, source_index, dead_flags):
    place = lax.axis_index("chan").astype(jnp.int32)
    mine = lax.axis_index("tm").astype(jnp.int32).reshape(1)
    live_all = 1.0 - dead_flags.astype(f32)
    live = lax.dynamic_slice_in_dim(live_all, place * WIDTH, WIDTH).reshape(1, WIDTH)
    place = place // 8 * 4 + place % 4
    own_sources = lax.dynamic_slice_in_dim(source_index, place * PICK, PICK)
    live_source = jnp.tile(live_all[own_sources], KW).reshape(KW * PICK, 1)
    table = dft_table()

    received = lax.all_to_all(encode(samples, source_index), "chan", 0, 0, tiled=True)
    pieces, spectra = transform(mine, received, table, live, 0, live_source)
    spectra = [spectra[0]] + [swap(spectra[k], "tm", TM, k) for k in range(1, TM)]
    first = [pieces[0]] + [swap(after(pieces[k], spectra[1]), "tm", TM, k) for k in range(1, TM)]
    packed = pack(spectra)
    groups = [[x * 8 + z * 4 + y for x in range(4) for y in range(4)] for z in range(2)]
    left = lax.all_to_all(packed, "chan", 0, 0, tiled=True, axis_index_groups=groups)
    pieces, _ = transform(mine, after(received, packed), table, live, 1)
    second = [pieces[0]] + [
        swap(pieces[k], "tm", TM, k) for k in range(1, TM)
    ]
    result = stack(left, first, 0, None)
    return stack(left, second, 1, result)


def solution(mesh):
    return jax.shard_map(
        shards,
        mesh=mesh,
        in_specs=(P("tm", "chan", None), P(), P()),
        out_specs=P("tm", None, None, "chan"),
        check_vma=False,
    )
```
